32 devices in a mesh: gx: 4 (over z), gy: 4 (over y, x), gz: 2 (over core).
Axes of the slice: x: 2, y: 2, z: 4, core: 2. Of those that a mesh axis runs over, the one named last changes fastest.
Arguments:
- source: bfloat16 [32, 1024, 1024], P('gx', 'gy', 'gz'), may hold values from -14 to 14
- observed: bfloat16 [32, 1024, 1024], P('gx', 'gy', 'gz'), may hold values from -14 to 14
- physics: float32 [3], replicated, may hold values from -8.5 to 0.5, as said below
- first_weight: float32 [3, 256], replicated, may hold values from -12 to 12
- first_bias: float32 [3, 256], replicated, may hold values from -8 to 8
- hidden_weight: float32 [3, 2, 256, 256], replicated, may hold values from -0.45 to 0.45
- hidden_bias: float32 [3, 2, 256], replicated, may hold values from -3 to 3
- final_weight: float32 [3, 256, 64], replicated, may hold values from -0.375 to 0.375
- final_bias: float32 [3, 64], replicated, may hold values from -3 to 3
Outputs:
- total_loss: float32 [], replicated
- physics_grad: float32 [3], replicated
- first_weight_grad: float32 [3, 256], replicated
- first_bias_grad: float32 [3, 256], replicated
- hidden_weight_grad: float32 [3, 2, 256, 256], replicated
- hidden_bias_grad: float32 [3, 2, 256], replicated
- final_weight_grad: float32 [3, 256, 64], replicated
- final_bias_grad: float32 [3, 64], replicated
The draws below stay inside these ranges and needn't reach their ends.
Inputs may be any that keep to these rules, and one draw needn't show every extreme that they name: physics[0] lies in -8.5 .. -7.0, physics[1] in 0.04 .. 0.16, physics[2] in -0.5 .. 0.5.
All inputs are finite; a program needn't handle non-finite values.
Results may differ from the reference program's by a relative error of at most 0.0003.
Values sent between devices are 32-bit elements; how exact they have to be, the bound alone decides.
A program may use at most 128 MiB of HBM per device.

```python
import math
import jax
import jax.numpy as jnp
from jax import lax

WIDTH = 256
RANK = 64
DEPTH = 2
CX = 8
NX = 32
NY = 1024
NZ = 1024


def axis_points(count):
    return (2 * jnp.arange(count) + 1).astype(jnp.float32) / count - 1.0


def wave_field(key):
    amp_key, phase_key = jax.random.split(key)
    amplitudes = jax.random.uniform(amp_key, (4,), jnp.float32, -1.0, 1.0)
    phases = jax.random.uniform(phase_key, (4, 3), jnp.float32, -math.pi, math.pi)
    x_axis = axis_points(NX)
    y_axis = axis_points(NY)
    z_axis = axis_points(NZ)
    field = jnp.zeros((NX, NY, NZ), jnp.float32)
    for mode_index in range(4):
        slow_rate = math.pi * (mode_index + 1) / 2.0
        fast_rate = math.pi * (10 + 4 * mode_index)
        y_rate = fast_rate if mode_index % 2 == 0 else slow_rate
        z_rate = slow_rate if mode_index % 2 == 0 else fast_rate
        x_wave = jnp.cos(slow_rate * x_axis + phases[mode_index, 0])
        y_wave = jnp.cos(y_rate * y_axis + phases[mode_index, 1])
        z_wave = jnp.cos(z_rate * z_axis + phases[mode_index, 2])
        field = field + amplitudes[mode_index] * x_wave[:, None, None] * y_wave[None, :, None] * z_wave[None, None, :]
    return field


def rough_planes(key):
    row_key, column_key = jax.random.split(key)
    rows = jax.random.uniform(row_key, (NY,), jnp.float32, 0.6, 1.5)
    columns = jax.random.uniform(column_key, (NZ,), jnp.float32, 0.6, 1.5)
    return rows[None, :, None] * columns[None, None, :]


def draw_source(key, part):
    key = jax.random.fold_in(key, 5)
    wave_key, rough_key, noise_key = jax.random.split(key, 3)
    smooth = wave_field(wave_key)
    rough = rough_planes(rough_key)
    noise = jax.random.uniform(noise_key, (NX, NY, NZ), jnp.float32, -0.5, 0.5)
    return (1.5 * smooth * rough + noise).astype(jnp.bfloat16)


def draw_observed(key, part):
    key = jax.random.fold_in(key, 9)
    wave_key, rough_key, noise_key = jax.random.split(key, 3)
    smooth = wave_field(wave_key)
    rough = rough_planes(rough_key)
    noise = jax.random.uniform(noise_key, (NX, NY, NZ), jnp.float32, -0.3, 0.3)
    return (1.5 * smooth * rough + noise).astype(jnp.bfloat16)


def draw_physics(key, part):
    key = jax.random.fold_in(key, 21)
    unit = jax.random.uniform(key, (3,), jnp.float32, 0.0, 1.0)
    return jnp.stack([-8.5 + 1.5 * unit[0], 0.04 + 0.12 * unit[1], -0.5 + unit[2]]).astype(jnp.float32)


def draw_hidden_weight(key, part):
    key = jax.random.fold_in(key, 17)
    sign_key, size_key = jax.random.split(key)
    shape = (3, DEPTH, WIDTH, WIDTH)
    signs = jax.random.randint(sign_key, shape, 0, 2).astype(jnp.float32) * 2.0 - 1.0
    sizes = jax.random.uniform(size_key, shape, jnp.float32, 0.3, 0.45)
    return (signs * sizes).astype(jnp.float32)


def normal_values(rng, shape, scale, bound, held_as=jnp.bfloat16):
    values = scale * jax.random.normal(rng, shape, jnp.float32)
    return jnp.clip(values, min=-bound, max=bound).astype(held_as)


def setup_inputs(seed: int = 0) -> dict:
    arg_keys = jax.random.split(jax.random.key(seed), 10)
    return {
        "source": draw_source(jax.random.fold_in(arg_keys[9], 71), 0),
        "observed": draw_observed(jax.random.fold_in(arg_keys[9], 71), 0),
        "physics": draw_physics(jax.random.fold_in(arg_keys[9], 71), 0),
        "first_weight": jnp.clip(jax.random.uniform(arg_keys[3], (3, WIDTH), jnp.float32, -12.0, 12.0), -12.0, 12.0),
        "first_bias": jnp.clip(jax.random.uniform(arg_keys[4], (3, WIDTH), jnp.float32, -8.0, 8.0), -8.0, 8.0),
        "hidden_weight": draw_hidden_weight(jax.random.fold_in(arg_keys[9], 71), 0),
        "hidden_bias": normal_values(arg_keys[6], (3, DEPTH, WIDTH), 0.5, 3.0, jnp.float32),
        "final_weight": normal_values(arg_keys[7], (3, WIDTH, RANK), WIDTH ** -0.5, 0.375, jnp.float32),
        "final_bias": normal_values(arg_keys[8], (3, RANK), 0.5, 3.0, jnp.float32),
    }


HIGHEST = lax.Precision.HIGHEST

def matmul_rows(left, right):
    return jnp.dot(left, right, precision=HIGHEST, preferred_element_type=jnp.float32)

def contract_last(left, right):
    return lax.dot_general(left, right, (((1,), (1,)), ((), ())), precision=HIGHEST, preferred_element_type=jnp.float32)

def contract_first(left, right):
    return lax.dot_general(left, right, (((0,), (0,)), ((), ())), precision=HIGHEST, preferred_element_type=jnp.float32)

def coordinates(offset, count, whole):
    position = offset + jnp.arange(count, dtype=jnp.int32)
    return (2 * position + 1).astype(jnp.float32) / whole - 1.0

def network_jets(points, first_weight, first_bias, hidden_weight, hidden_bias, final_weight, final_bias):
    count = points.shape[0]
    pre_act = points[:, None] * first_weight[None, :] + first_bias[None, :]
    hidden = jnp.tanh(pre_act)
    damping = 1.0 - hidden * hidden
    slope = damping * first_weight[None, :]
    curve = -2.0 * hidden * damping * (first_weight * first_weight)[None, :]
    for depth_index in range(hidden_weight.shape[0]):
        stacked = matmul_rows(jnp.concatenate([hidden, slope, curve], 0), hidden_weight[depth_index])
        pre_act = stacked[:count] + hidden_bias[depth_index][None, :]
        pre_slope = stacked[count:2 * count]
        pre_curve = stacked[2 * count:]
        hidden = jnp.tanh(pre_act)
        damping = 1.0 - hidden * hidden
        slope = damping * pre_slope
        curve = damping * pre_curve - 2.0 * hidden * damping * pre_slope * pre_slope
    stacked = matmul_rows(jnp.concatenate([hidden, slope, curve], 0), final_weight)
    return (stacked[:count] + final_bias[None, :], stacked[count:2 * count], stacked[2 * count:])

def network_grads(points, weights, cotangents):
    outputs, pullback = jax.vjp(lambda params: network_jets(points, *params), weights)
    return pullback(cotangents)[0]

def block_terms(x_jets, y_jets, z_jets, y_points, z_points, source, observed, physics, ncells):
    x_value, x_slope, x_curve = x_jets
    y_value, y_curve = y_jets
    z_value, z_curve = z_jets
    x_count, rank = x_value.shape
    y_count = y_value.shape[0]
    z_count = z_value.shape[0]
    plane = x_count * y_count
    pair_value = (x_value[:, None, :] * y_value[None, :, :]).reshape(plane, rank)
    pair_slope = (x_slope[:, None, :] * y_value[None, :, :]).reshape(plane, rank)
    pair_curve = (x_curve[:, None, :] * y_value[None, :, :] + x_value[:, None, :] * y_curve[None, :, :]).reshape(plane, rank)
    pair_rows = jnp.concatenate([pair_value, pair_slope], 0)
    pair_lap = jnp.concatenate([pair_curve, pair_value], 1)
    z_both = jnp.concatenate([z_value, z_curve], 1)
    forward = contract_last(pair_rows, z_value)
    solution = forward[:plane].reshape(x_count, y_count, z_count)
    along_x = forward[plane:].reshape(x_count, y_count, z_count)
    laplace = contract_last(pair_lap, z_both).reshape(x_count, y_count, z_count)
    diffusivity = jnp.exp(physics[0])
    peak_speed = physics[1]
    bend_rate = physics[2]
    y_square = y_points * y_points
    z_square = z_points * z_points
    base = (1.0 - y_square)[:, None] * (1.0 - z_square)[None, :]
    spread = y_square[:, None] + z_square[None, :]
    profile = base * (1.0 + bend_rate * spread)
    speed = peak_speed * profile
    residual = speed[None] * along_x - diffusivity * laplace - source.astype(jnp.float32)
    misfit = solution - observed.astype(jnp.float32)
    weighted = 2.0 * residual / ncells
    scalars = jnp.stack([(jnp.sum(residual * residual) + jnp.sum(misfit * misfit)) / ncells, -diffusivity * jnp.sum(weighted * laplace), jnp.sum(weighted * along_x * profile[None]), peak_speed * jnp.sum(weighted * along_x * (base * spread)[None])])
    field_rows = jnp.concatenate([(2.0 * misfit / ncells).reshape(plane, z_count), (weighted * speed[None]).reshape(plane, z_count)], 0)
    curve_rows = (-diffusivity * weighted).reshape(plane, z_count)
    along_z = matmul_rows(field_rows, z_value)
    curve_z = matmul_rows(curve_rows, z_both)
    cross_value = along_z[:plane].reshape(x_count, y_count, rank)
    cross_slope = along_z[plane:].reshape(x_count, y_count, rank)
    cross_curve = curve_z[:, :rank].reshape(x_count, y_count, rank)
    cross_bend = curve_z[:, rank:].reshape(x_count, y_count, rank)
    x_grad = (lax.optimization_barrier(jnp.sum(cross_value * y_value[None] + cross_curve * y_curve[None] + cross_bend * y_value[None], 1)), lax.optimization_barrier(jnp.sum(cross_slope * y_value[None], 1)), lax.optimization_barrier(jnp.sum(cross_curve * y_value[None], 1)))
    y_grad = (lax.optimization_barrier(jnp.sum(cross_value * x_value[:, None] + cross_slope * x_slope[:, None] + cross_curve * x_curve[:, None] + cross_bend * x_value[:, None], 0)), lax.optimization_barrier(jnp.sum(cross_curve * x_value[:, None], 0)))
    z_lap = contract_first(curve_rows, pair_lap)
    z_grad = (contract_first(field_rows, pair_rows) + z_lap[:, :rank], z_lap[:, rank:])
    return (scalars, x_grad, y_grad, z_grad)

def reference(source, observed, physics, first_weight, first_bias, hidden_weight, hidden_bias, final_weight, final_bias):

    def weights_of(which):
        return (first_weight[which], first_bias[which], hidden_weight[which], hidden_bias[which], final_weight[which], final_bias[which])
    ncells = float(NX * NY * NZ)
    x_points = coordinates(0, NX, NX)
    y_points = coordinates(0, NY, NY)
    z_points = coordinates(0, NZ, NZ)
    x_jets = network_jets(x_points, *weights_of(0))
    y_jets = network_jets(y_points, *weights_of(1))
    z_jets = network_jets(z_points, *weights_of(2))
    blocks = NX // CX
    pieces = (source.reshape(blocks, CX, NY, NZ), observed.reshape(blocks, CX, NY, NZ), x_jets[0].reshape(blocks, CX, RANK), x_jets[1].reshape(blocks, CX, RANK), x_jets[2].reshape(blocks, CX, RANK))

    def scan_step(carry, piece):
        scalars, x_grad, y_grad, z_grad = block_terms((piece[2], piece[3], piece[4]), (y_jets[0], y_jets[2]), (z_jets[0], z_jets[2]), y_points, z_points, piece[0], piece[1], physics, ncells)
        carry = (carry[0] + scalars, carry[1] + y_grad[0], carry[2] + y_grad[1], carry[3] + z_grad[0], carry[4] + z_grad[1])
        return (carry, x_grad)
    start = (jnp.zeros((4,), jnp.float32), jnp.zeros((NY, RANK), jnp.float32), jnp.zeros((NY, RANK), jnp.float32), jnp.zeros((NZ, RANK), jnp.float32), jnp.zeros((NZ, RANK), jnp.float32))
    carry, x_stack = lax.scan(scan_step, start, pieces)
    x_cot = (x_stack[0].reshape(NX, RANK), x_stack[1].reshape(NX, RANK), x_stack[2].reshape(NX, RANK))
    x_grads = network_grads(x_points, weights_of(0), x_cot)
    y_grads = network_grads(y_points, weights_of(1), (carry[1], jnp.zeros_like(carry[1]), carry[2]))
    z_grads = network_grads(z_points, weights_of(2), (carry[3], jnp.zeros_like(carry[3]), carry[4]))
    grads = [jnp.stack([x_grads[slot], y_grads[slot], z_grads[slot]]) for slot in range(6)]
    totals = carry[0]
    return (totals[0], totals[1:4], grads[0], grads[1], grads[2], grads[3], grads[4], grads[5])
```

```python
import functools
import jax
import jax.numpy as jnp
from jax import lax
from jax.experimental import pallas as pl
from jax.experimental.pallas import tpu as pltpu
from jax.sharding import PartitionSpec as P

HIGHEST = lax.Precision.HIGHEST


def matmul_rows(left, right):
    return jnp.dot(left, right, precision=HIGHEST, preferred_element_type=jnp.float32)


def contract_last(left, right):
    return lax.dot_general(
        left, right, (((1,), (1,)), ((), ())), precision=HIGHEST, preferred_element_type=jnp.float32
    )


def contract_first(left, right):
    return lax.dot_general(
        left, right, (((0,), (0,)), ((), ())), precision=HIGHEST, preferred_element_type=jnp.float32
    )


def matmul_rows_high(left, right):
    return jnp.dot(left, right, precision=lax.Precision.HIGH, preferred_element_type=jnp.float32)


def contract_last_high(left, right):
    return lax.dot_general(
        left, right, (((1,), (1,)), ((), ())), precision=lax.Precision.HIGH, preferred_element_type=jnp.float32
    )


def contract_first_high(left, right):
    return lax.dot_general(
        left, right, (((0,), (0,)), ((), ())), precision=lax.Precision.HIGH, preferred_element_type=jnp.float32
    )


def coordinates(offset, count, whole):
    position = offset + jnp.arange(count, dtype=jnp.int32)
    return (2 * position + 1).astype(jnp.float32) / whole - 1.0


def network_jets(
    points, first_weight, first_bias, hidden_weight, hidden_bias, final_weight, final_bias
):
    count = points.shape[0]
    pre_act = points[:, None] * first_weight[None, :] + first_bias[None, :]
    hidden = jnp.tanh(pre_act)
    damping = 1.0 - hidden * hidden
    slope = damping * first_weight[None, :]
    curve = -2.0 * hidden * damping * (first_weight * first_weight)[None, :]
    for depth_index in range(hidden_weight.shape[0]):
        stacked = matmul_rows(
            jnp.concatenate([hidden, slope, curve], 0), hidden_weight[depth_index]
        )
        pre_act = stacked[:count] + hidden_bias[depth_index][None, :]
        pre_slope = stacked[count : 2 * count]
        pre_curve = stacked[2 * count :]
        hidden = jnp.tanh(pre_act)
        damping = 1.0 - hidden * hidden
        slope = damping * pre_slope
        curve = damping * pre_curve - 2.0 * hidden * damping * pre_slope * pre_slope
    stacked = matmul_rows(jnp.concatenate([hidden, slope, curve], 0), final_weight)
    return (stacked[:count] + final_bias[None, :], stacked[count : 2 * count], stacked[2 * count :])


def network_grads(points, weights, cotangents):
    outputs, pullback = jax.vjp(lambda params: network_jets(points, *params), weights)
    return pullback(cotangents)[0]


def block_terms(x_jets, y_jets, z_jets, y_points, z_points, source, observed, physics, ncells):
    x_value, x_slope, x_curve = x_jets
    y_value, y_curve = y_jets
    z_value, z_curve = z_jets
    x_count, rank = x_value.shape
    y_count = y_value.shape[0]
    z_count = z_value.shape[0]
    plane = x_count * y_count
    pair_value = (x_value[:, None, :] * y_value[None, :, :]).reshape(plane, rank)
    pair_slope = (x_slope[:, None, :] * y_value[None, :, :]).reshape(plane, rank)
    pair_curve = (
        x_curve[:, None, :] * y_value[None, :, :] + x_value[:, None, :] * y_curve[None, :, :]
    ).reshape(plane, rank)
    pair_rows = jnp.concatenate([pair_value, pair_slope], 0)
    pair_lap = jnp.concatenate([pair_curve, pair_value], 1)
    z_both = jnp.concatenate([z_value, z_curve], 1)
    forward = contract_last_high(pair_rows, z_value)
    solution = forward[:plane].reshape(x_count, y_count, z_count)
    along_x = forward[plane:].reshape(x_count, y_count, z_count)
    laplace = contract_last_high(pair_lap, z_both).reshape(x_count, y_count, z_count)
    diffusivity = jnp.exp(physics[0])
    peak_speed = physics[1]
    bend_rate = physics[2]
    y_square = y_points * y_points
    z_square = z_points * z_points
    base = (1.0 - y_square)[:, None] * (1.0 - z_square)[None, :]
    spread = y_square[:, None] + z_square[None, :]
    profile = base * (1.0 + bend_rate * spread)
    speed = peak_speed * profile
    residual = speed[None] * along_x - diffusivity * laplace - source.astype(jnp.float32)
    misfit = solution - observed.astype(jnp.float32)
    weighted = 2.0 * residual / ncells
    scalars = jnp.stack(
        [
            (jnp.sum(residual * residual) + jnp.sum(misfit * misfit)) / ncells,
            -diffusivity * jnp.sum(weighted * laplace),
            jnp.sum(weighted * along_x * profile[None]),
            peak_speed * jnp.sum(weighted * along_x * (base * spread)[None]),
        ]
    )
    field_rows = jnp.concatenate(
        [
            (2.0 * misfit / ncells).reshape(plane, z_count),
            (weighted * speed[None]).reshape(plane, z_count),
        ],
        0,
    )
    curve_rows = (-diffusivity * weighted).reshape(plane, z_count)
    along_z = matmul_rows_high(field_rows, z_value)
    curve_z = matmul_rows_high(curve_rows, z_both)
    cross_value = along_z[:plane].reshape(x_count, y_count, rank)
    cross_slope = along_z[plane:].reshape(x_count, y_count, rank)
    cross_curve = curve_z[:, :rank].reshape(x_count, y_count, rank)
    cross_bend = curve_z[:, rank:].reshape(x_count, y_count, rank)
    x_grad = (
        jnp.sum(
            cross_value * y_value[None] + cross_curve * y_curve[None] + cross_bend * y_value[None],
            1,
        ),
        jnp.sum(cross_slope * y_value[None], 1),
        jnp.sum(cross_curve * y_value[None], 1),
    )
    y_grad = (
        jnp.sum(
            cross_value * x_value[:, None]
            + cross_slope * x_slope[:, None]
            + cross_curve * x_curve[:, None]
            + cross_bend * x_value[:, None],
            0,
        ),
        jnp.sum(cross_curve * x_value[:, None], 0),
    )
    z_lap = contract_first_high(curve_rows, pair_lap)
    z_grad = (contract_first_high(field_rows, pair_rows) + z_lap[:, :rank], z_lap[:, rank:])
    return (scalars, x_grad, y_grad, z_grad)


def stack_three(x_grads, y_grads, z_grads):
    return [jnp.stack([x_grads[slot], y_grads[slot], z_grads[slot]]) for slot in range(6)]


LANES = 256
MESH_ID = pl.DeviceIdType.MESH


def reduce_plan(total_rows, sizes):
    devices = 1
    for size in sizes.values():
        devices *= size
    unit = 8 * devices
    units = -(-total_rows // unit)
    lead = max(1, (units * 7 + 5) // 10)
    if lead == units and units > 1:
        lead -= 1
    channels = [(0, lead * unit, ("gz", "gy", "gx"))]
    if units > lead:
        channels.append((lead * unit, (units - lead) * unit, ("gz", "gx", "gy")))
    return units * unit, channels


def all_reduce_body(channels, sizes, in_ref, out_ref, recv_refs, work_refs, sems):
    places = {name: lax.axis_index(name) for name in sizes}

    def partner(name, step):
        return {name: lax.rem(places[name] + step, sizes[name])}

    phases = len(sizes)
    sources = [in_ref] * len(channels)
    starts = [first for first, _, _ in channels]
    lengths = [rows for _, rows, _ in channels]
    bases = [first for first, _, _ in channels]
    history = [[] for _ in channels]
    for phase in range(phases):
        flights = []
        for slot, (_, _, order) in enumerate(channels):
            name = order[phase]
            part = lengths[slot] // sizes[name]
            for step in range(1, sizes[name]):
                peer = lax.rem(places[name] + step, sizes[name])
                copy = pltpu.make_async_remote_copy(
                    src_ref=sources[slot].at[pl.ds(pl.multiple_of(starts[slot] + peer * part, 8), part)],
                    dst_ref=recv_refs[slot][phase].at[step - 1],
                    send_sem=sems[slot][0].at[phase, step - 1],
                    recv_sem=sems[slot][1].at[phase, step - 1],
                    device_id=partner(name, step),
                    device_id_type=MESH_ID,
                )
                copy.start()
                flights.append((slot, copy))
        for slot, (_, _, order) in enumerate(channels):
            name = order[phase]
            part = lengths[slot] // sizes[name]
            for owner, copy in flights:
                if owner == slot:
                    copy.wait()
            mine = pl.multiple_of(starts[slot] + places[name] * part, 8)
            value = sources[slot][pl.ds(mine, part)]
            for step in range(1, sizes[name]):
                value = value + recv_refs[slot][phase][step - 1]
            history[slot].append((name, bases[slot], part))
            bases[slot] = pl.multiple_of(bases[slot] + places[name] * part, 8)
            if phase == phases - 1:
                out_ref[pl.ds(bases[slot], part)] = value
            else:
                work_refs[slot][phase][...] = value
                sources[slot] = work_refs[slot][phase]
                starts[slot] = 0
            lengths[slot] = part
    for phase in reversed(range(phases)):
        flights = []
        for slot in range(len(channels)):
            name, base, part = history[slot][phase]
            mine = out_ref.at[pl.ds(pl.multiple_of(base + places[name] * part, 8), part)]
            for step in range(1, sizes[name]):
                copy = pltpu.make_async_remote_copy(
                    src_ref=mine,
                    dst_ref=mine,
                    send_sem=sems[slot][2].at[phase, step - 1],
                    recv_sem=sems[slot][3].at[phase, step - 1],
                    device_id=partner(name, step),
                    device_id_type=MESH_ID,
                )
                copy.start()
                flights.append(copy)
        for copy in flights:
            copy.wait()


def entry_barrier(sizes):
    barrier = pltpu.get_barrier_semaphore()
    count = 0
    for name, size in sizes.items():
        for step in range(1, size):
            peer = lax.rem(lax.axis_index(name) + step, size)
            pl.semaphore_signal(barrier, inc=1, device_id={name: peer}, device_id_type=MESH_ID)
            count += 1
    pl.semaphore_wait(barrier, count)


def reduce_scratch(channels, sizes):
    scratch = []
    widest = max(sizes.values())
    for _, rows, order in channels:
        for name in order:
            rows //= sizes[name]
            scratch.append(pltpu.VMEM((sizes[name] - 1, rows, LANES), jnp.float32))
            scratch.append(pltpu.VMEM((rows, LANES), jnp.float32))
        for _ in range(4):
            scratch.append(pltpu.SemaphoreType.DMA((len(sizes), widest - 1)))
    return scratch


def split_scratch(channels, sizes, refs):
    phases = len(sizes)
    each = 2 * phases + 4
    recv_refs, work_refs, sems = [], [], []
    for slot in range(len(channels)):
        group = refs[slot * each : (slot + 1) * each]
        recv_refs.append(group[0 : 2 * phases : 2])
        work_refs.append(group[1 : 2 * phases : 2])
        sems.append(group[2 * phases :])
    return recv_refs, work_refs, sems


def reduce_kernel(channels, sizes, in_ref, out_ref, *scratch):
    entry_barrier(sizes)
    all_reduce_body(channels, sizes, in_ref, out_ref, *split_scratch(channels, sizes, scratch))


def all_reduce(packed, channels, sizes):
    return pl.pallas_call(
        functools.partial(reduce_kernel, channels, sizes),
        out_shape=jax.ShapeDtypeStruct(packed.shape, jnp.float32),
        in_specs=[pl.BlockSpec(memory_space=pltpu.VMEM)],
        out_specs=pl.BlockSpec(memory_space=pltpu.VMEM),
        scratch_shapes=reduce_scratch(channels, sizes),
        compiler_params=pltpu.CompilerParams(collective_id=0, has_side_effects=True, vmem_limit_bytes=24 << 20),
    )(packed)


def local(
    source,
    observed,
    physics,
    first_weight,
    first_bias,
    hidden_weight,
    hidden_bias,
    final_weight,
    final_bias,
):

    def weights_of(which):
        return (
            first_weight[which],
            first_bias[which],
            hidden_weight[which],
            hidden_bias[which],
            final_weight[which],
            final_bias[which],
        )

    x_count, y_count, z_count = source.shape
    x_whole = x_count * lax.axis_size("gx")
    y_whole = y_count * lax.axis_size("gy")
    z_whole = z_count * lax.axis_size("gz")
    ncells = float(x_whole * y_whole * z_whole)
    x_points = coordinates(lax.axis_index("gx") * x_count, x_count, x_whole)
    y_points = coordinates(lax.axis_index("gy") * y_count, y_count, y_whole)
    z_points = coordinates(lax.axis_index("gz") * z_count, z_count, z_whole)
    x_jets = network_jets(x_points, *weights_of(0))
    y_jets = network_jets(y_points, *weights_of(1))
    z_jets = network_jets(z_points, *weights_of(2))
    scalars, x_cot, y_cot, z_cot = block_terms(
        x_jets,
        (y_jets[0], y_jets[2]),
        (z_jets[0], z_jets[2]),
        y_points,
        z_points,
        source,
        observed,
        physics,
        ncells,
    )
    x_grads = network_grads(x_points, weights_of(0), (x_cot[0], x_cot[1], x_cot[2]))
    y_grads = network_grads(y_points, weights_of(1), (y_cot[0], jnp.zeros_like(y_cot[0]), y_cot[1]))
    z_grads = network_grads(z_points, weights_of(2), (z_cot[0], jnp.zeros_like(z_cot[0]), z_cot[1]))
    stacked = stack_three(x_grads, y_grads, z_grads)
    sizes = {name: lax.axis_size(name) for name in ("gx", "gy", "gz")}
    pieces = [
        stacked[2].reshape(-1, LANES),
        jnp.swapaxes(stacked[4], 1, 2).reshape(-1, LANES),
        stacked[0],
        stacked[1],
        stacked[3].reshape(-1, LANES),
        jnp.pad(stacked[5], ((0, 0), (0, LANES - stacked[5].shape[1]))),
        jnp.pad(scalars[None], ((0, 0), (0, LANES - 4))),
    ]
    rows = sum(piece.shape[0] for piece in pieces)
    padded, channels = reduce_plan(rows, sizes)
    pieces.append(jnp.zeros((padded - rows, LANES), jnp.float32))
    summed = all_reduce(jnp.concatenate(pieces, 0), channels, sizes)
    parts = []
    start = 0
    for piece in pieces:
        parts.append(summed[start : start + piece.shape[0]])
        start += piece.shape[0]
    rank = final_weight.shape[2]
    return (
        parts[6][0, 0],
        parts[6][0, 1:4],
        parts[2],
        parts[3],
        parts[0].reshape(hidden_weight.shape),
        parts[4].reshape(hidden_bias.shape),
        jnp.swapaxes(parts[1].reshape(3, rank, LANES), 1, 2),
        parts[5][:, :rank],
    )


def solution(mesh):
    in_specs = (P("gx", "gy", "gz"), P("gx", "gy", "gz"), P(), P(), P(), P(), P(), P(), P())
    out_specs = (P(), P(), P(), P(), P(), P(), P(), P())
    return jax.shard_map(local, mesh=mesh, in_specs=in_specs, out_specs=out_specs, check_vma=False)
```

```python
import functools
import jax
import jax.numpy as jnp
from jax import lax
from jax.experimental import pallas as pl
from jax.experimental.pallas import tpu as pltpu
from jax.sharding import PartitionSpec as P

HIGHEST = lax.Precision.HIGHEST
CHUNK = 128

LANES = 256
MESH_ID = pl.DeviceIdType.MESH


def reduce_plan(total_rows, sizes):
    devices = 1
    for size in sizes.values():
        devices *= size
    unit = 8 * devices
    units = -(-total_rows // unit)
    lead = max(1, (units * 7 + 5) // 10)
    if lead == units and units > 1:
        lead -= 1
    channels = [(0, lead * unit, ("gz", "gy", "gx"))]
    if units > lead:
        channels.append((lead * unit, (units - lead) * unit, ("gz", "gx", "gy")))
    return units * unit, channels


def all_reduce_body(channels, sizes, in_ref, out_ref, recv_refs, work_refs, sems):
    places = {name: lax.axis_index(name) for name in sizes}

    def partner(name, step):
        return {name: lax.rem(places[name] + step, sizes[name])}

    phases = len(sizes)
    sources = [in_ref] * len(channels)
    starts = [first for first, _, _ in channels]
    lengths = [rows for _, rows, _ in channels]
    bases = [first for first, _, _ in channels]
    history = [[] for _ in channels]
    for phase in range(phases):
        flights = []
        for slot, (_, _, order) in enumerate(channels):
            name = order[phase]
            part = lengths[slot] // sizes[name]
            for step in range(1, sizes[name]):
                peer = lax.rem(places[name] + step, sizes[name])
                copy = pltpu.make_async_remote_copy(
                    src_ref=sources[slot].at[pl.ds(pl.multiple_of(starts[slot] + peer * part, 8), part)],
                    dst_ref=recv_refs[slot][phase].at[step - 1],
                    send_sem=sems[slot][0].at[phase, step - 1],
                    recv_sem=sems[slot][1].at[phase, step - 1],
                    device_id=partner(name, step),
                    device_id_type=MESH_ID,
                )
                copy.start()
                flights.append((slot, copy))
        for slot, (_, _, order) in enumerate(channels):
            name = order[phase]
            part = lengths[slot] // sizes[name]
            for owner, copy in flights:
                if owner == slot:
                    copy.wait()
            mine = pl.multiple_of(starts[slot] + places[name] * part, 8)
            value = sources[slot][pl.ds(mine, part)]
            for step in range(1, sizes[name]):
                value = value + recv_refs[slot][phase][step - 1]
            history[slot].append((name, bases[slot], part))
            bases[slot] = pl.multiple_of(bases[slot] + places[name] * part, 8)
            if phase == phases - 1:
                out_ref[pl.ds(bases[slot], part)] = value
            else:
                work_refs[slot][phase][...] = value
                sources[slot] = work_refs[slot][phase]
                starts[slot] = 0
            lengths[slot] = part
    for phase in reversed(range(phases)):
        flights = []
        for slot in range(len(channels)):
            name, base, part = history[slot][phase]
            mine = out_ref.at[pl.ds(pl.multiple_of(base + places[name] * part, 8), part)]
            for step in range(1, sizes[name]):
                copy = pltpu.make_async_remote_copy(
                    src_ref=mine,
                    dst_ref=mine,
                    send_sem=sems[slot][2].at[phase, step - 1],
                    recv_sem=sems[slot][3].at[phase, step - 1],
                    device_id=partner(name, step),
                    device_id_type=MESH_ID,
                )
                copy.start()
                flights.append(copy)
        for copy in flights:
            copy.wait()


def entry_barrier(sizes):
    barrier = pltpu.get_barrier_semaphore()
    count = 0
    for name, size in sizes.items():
        for step in range(1, size):
            peer = lax.rem(lax.axis_index(name) + step, size)
            pl.semaphore_signal(barrier, inc=1, device_id={name: peer}, device_id_type=MESH_ID)
            count += 1
    pl.semaphore_wait(barrier, count)


def reduce_scratch(channels, sizes):
    scratch = []
    widest = max(sizes.values())
    for _, rows, order in channels:
        for name in order:
            rows //= sizes[name]
            scratch.append(pltpu.VMEM((sizes[name] - 1, rows, LANES), jnp.float32))
            scratch.append(pltpu.VMEM((rows, LANES), jnp.float32))
        for _ in range(4):
            scratch.append(pltpu.SemaphoreType.DMA((len(sizes), widest - 1)))
    return scratch


def split_scratch(channels, sizes, refs):
    phases = len(sizes)
    each = 2 * phases + 4
    recv_refs, work_refs, sems = [], [], []
    for slot in range(len(channels)):
        group = refs[slot * each : (slot + 1) * each]
        recv_refs.append(group[0 : 2 * phases : 2])
        work_refs.append(group[1 : 2 * phases : 2])
        sems.append(group[2 * phases :])
    return recv_refs, work_refs, sems


def reduce_kernel(channels, sizes, in_ref, out_ref, *scratch):
    entry_barrier(sizes)
    all_reduce_body(channels, sizes, in_ref, out_ref, *split_scratch(channels, sizes, scratch))


def all_reduce(packed, channels, sizes):
    return pl.pallas_call(
        functools.partial(reduce_kernel, channels, sizes),
        out_shape=jax.ShapeDtypeStruct(packed.shape, jnp.float32),
        in_specs=[pl.BlockSpec(memory_space=pltpu.VMEM)],
        out_specs=pl.BlockSpec(memory_space=pltpu.VMEM),
        scratch_shapes=reduce_scratch(channels, sizes),
        compiler_params=pltpu.CompilerParams(collective_id=0, has_side_effects=True, vmem_limit_bytes=24 << 20),
    )(packed)


F32 = jnp.float32
BF16 = jnp.bfloat16


def split(value):
    high = value.astype(BF16)
    return high, (value - high.astype(F32)).astype(BF16)


def product(left, right, dims):
    return lax.dot_general(left, right, (dims, ((), ())), preferred_element_type=F32)


def three_pass(left, right, dims):
    left_high, left_low = left
    right_high, right_low = right
    return (
        product(left_high, right_high, dims)
        + product(left_low, right_high, dims)
        + product(left_high, right_low, dims)
    )


LAST = ((1,), (1,))
FIRST = ((0,), (0,))
PLAIN = ((1,), (0,))


def tanh_jet(hidden, pre_slope, pre_curve):
    damping = 1.0 - hidden * hidden
    slope = damping * pre_slope
    if pre_curve is None:
        return slope, -2.0 * hidden * damping * (pre_slope * pre_slope)
    return slope, damping * pre_curve - 2.0 * hidden * damping * pre_slope * pre_slope


def tanh_jet_back(hidden, pre_slope, pre_curve, d_value, d_slope, d_curve):
    damping = 1.0 - hidden * hidden
    square = pre_slope * pre_slope
    d_pre_curve = damping * d_curve
    d_pre_slope = -4.0 * hidden * pre_slope * d_pre_curve
    bend = -2.0 * hidden * square
    if pre_curve is not None:
        bend = bend + pre_curve
    d_damping = bend * d_curve
    if d_slope is not None:
        d_pre_slope = d_pre_slope + damping * d_slope
        d_damping = d_damping + pre_slope * d_slope
    d_pre = damping * (d_value - 2.0 * square * d_pre_curve - 2.0 * hidden * d_damping)
    return d_pre, d_pre_slope, d_pre_curve


def points_column(offset, count, whole):
    position = offset + lax.broadcasted_iota(jnp.int32, (count, LANES), 0)
    return (2 * position + 1).astype(F32) * (1.0 / whole) - 1.0


def net_forward(which, points, first_row, count, refs):
    first_weight, first_bias, hidden_weight, hidden_bias, twice, bias_twice, hid, slo, cur = refs
    rows = pl.ds(first_row, count)
    weight = first_weight[which]
    hidden = jnp.tanh(points * weight + first_bias[which])
    hid[0, rows] = hidden
    slope, curve = tanh_jet(hidden, weight, None)
    depth = hidden_weight.shape[1]
    for layer in range(depth):
        stacked = jnp.dot(
            jnp.concatenate([hidden, slope, curve], 0),
            hidden_weight[which, layer],
            precision=HIGHEST,
            preferred_element_type=F32,
        )
        pre_slope = stacked[count : 2 * count]
        pre_curve = stacked[2 * count :]
        hidden = jnp.tanh(stacked[:count] + hidden_bias[which * depth + layer])
        hid[layer + 1, rows] = hidden
        slo[layer, rows] = pre_slope
        cur[layer, rows] = pre_curve
        slope, curve = tanh_jet(hidden, pre_slope, pre_curve)
    stacked = jnp.dot(
        jnp.concatenate([hidden, slope, curve], 0), twice[which], precision=HIGHEST, preferred_element_type=F32
    )
    return (
        stacked[:count] + bias_twice[which],
        stacked[count : 2 * count],
        stacked[2 * count :],
    )


def row_sum(value):
    return jnp.sum(value, 0, keepdims=True)


def net_backward(which, points, first_row, count, refs, out_ref, small, cotangents, packed, rank):
    first_weight, first_bias, hidden_weight, hidden_bias, twice, bias_twice, hid, slo, cur = refs
    depth = hidden_weight.shape[1]
    width = LANES
    rows = pl.ds(first_row, count)
    at_final = 3 * depth * width
    lane = lax.broadcasted_iota(jnp.int32, (width, 2 * rank), 1)
    low_weight = split(jnp.where(lane < rank, twice[which], 0.0))
    high_weight = split(jnp.where(lane >= rank, twice[which], 0.0)) if packed else low_weight
    hidden = hid[depth, rows]
    pre_slope = slo[depth - 1, rows]
    pre_curve = cur[depth - 1, rows]
    slope, curve = tanh_jet(hidden, pre_slope, pre_curve)
    parts = [None if cot is None else split(cot) for cot in cotangents]
    grad = three_pass(parts[0], split(hidden), FIRST)[:rank]
    curve_grad = three_pass(parts[2], split(curve), FIRST)
    grad = grad + (curve_grad[rank:] if packed else curve_grad[:rank])
    d_value = three_pass(parts[0], low_weight, LAST)
    d_curve = three_pass(parts[2], high_weight, LAST)
    d_slope = None
    if parts[1] is not None:
        grad = grad + three_pass(parts[1], split(slope), FIRST)[:rank]
        d_slope = three_pass(parts[1], low_weight, LAST)
    out_ref[pl.ds(pl.multiple_of(at_final + which * rank, 8), rank)] += grad
    biases = row_sum(cotangents[0])
    small[6 + 3 * depth + which, :, 0 : 2 * rank] += biases
    for layer in reversed(range(depth)):
        steps = tanh_jet_back(hidden, pre_slope, pre_curve, d_value, d_slope, d_curve)
        small[6 + which * depth + layer] += row_sum(steps[0])
        hidden = hid[layer, rows]
        if layer:
            pre_slope = slo[layer - 1, rows]
            pre_curve = cur[layer - 1, rows]
        else:
            pre_slope = first_weight[which]
            pre_curve = None
        slope, curve = tanh_jet(hidden, pre_slope, pre_curve)
        deltas = split(jnp.concatenate(steps, 0))
        acts = split(jnp.concatenate([hidden, slope, curve], 0))
        out_ref[pl.ds(pl.multiple_of((which * depth + layer) * width, 8), width)] += three_pass(acts, deltas, FIRST)
        back = three_pass(deltas, split(hidden_weight[which, layer]), LAST)
        d_value, d_slope, d_curve = back[:count], back[count : 2 * count], back[2 * count :]
    steps = tanh_jet_back(hidden, pre_slope, None, d_value, d_slope, d_curve)
    small[which] += row_sum(points * steps[0] + steps[1])
    small[3 + which] += row_sum(steps[0])


def step_kernel(
    wholes,
    rank,
    offsets,
    physics,
    source,
    observed,
    first_weight,
    first_bias,
    hidden_weight,
    hidden_bias,
    twice,
    bias_twice,
    out_ref,
    hid,
    slo,
    cur,
    x_rows,
    x_cols,
    y_value,
    y_both,
    y_swap,
    y_turn,
    z_first,
    z_lap,
    z_high,
    z_low,
    speed_ref,
    profile_ref,
    shape_ref,
    u_ref,
    s_ref,
    l_ref,
    f_high,
    f_low,
    x_cot,
    y_cot,
    z_turn,
    sums,
    small,
):
    refs = (first_weight, first_bias, hidden_weight, hidden_bias, twice, bias_twice, hid, slo, cur)
    x_count, y_count, z_count = source.shape
    x_whole, y_whole, z_whole = wholes
    ncells = float(x_whole * y_whole * z_whole)
    wide = 2 * rank
    out_ref[...] = jnp.zeros_like(out_ref)
    small[...] = jnp.zeros_like(small)
    y_chunks = y_count // CHUNK
    z_chunks = z_count // CHUNK
    x_base = y_count + z_count
    lane = lax.broadcasted_iota(jnp.int32, (CHUNK, wide), 1)
    low = lane < rank

    def line_points(chunk):
        on_z = chunk >= y_chunks
        first = jnp.where(on_z, offsets[2] + (chunk - y_chunks) * CHUNK, offsets[1] + chunk * CHUNK)
        scale = jnp.where(on_z, F32(1.0 / z_whole), F32(1.0 / y_whole))
        position = first + lax.broadcasted_iota(jnp.int32, (CHUNK, LANES), 0)
        return (2 * position + 1).astype(F32) * scale - 1.0

    x_points = points_column(offsets[0], x_count, x_whole)
    x_jets = net_forward(0, x_points, x_base, x_count, refs)
    for slot in range(3):
        for row in range(x_count):
            x_rows[row, :, slot * wide : (slot + 1) * wide] = x_jets[slot][row : row + 1]
    for slot in range(3):
        turned = jnp.transpose(
            jnp.concatenate([x_jets[slot], jnp.zeros((CHUNK - x_count, wide), F32)], 0)
        )
        for row in range(x_count):
            x_cols[row, slot * rank : (slot + 1) * rank] = jnp.broadcast_to(
                turned[:rank, row : row + 1], (rank, CHUNK)
            )

    def forward_chunk(chunk, carry):
        which = jnp.where(chunk >= y_chunks, 2, 1)
        start = pl.multiple_of(chunk * CHUNK, CHUNK)
        value, _, curve = net_forward(which, line_points(chunk), start, CHUNK, refs)
        both = jnp.where(low, value, curve)

        @pl.when(chunk < y_chunks)
        def _():
            rows = pl.ds(start, CHUNK)
            y_value[rows] = value
            y_both[rows] = both
            y_swap[rows] = jnp.where(low, curve, value)
            turned = jnp.transpose(both)
            for half in range(y_chunks):
                @pl.when(chunk == half)
                def _():
                    y_turn[:, half * CHUNK : (half + 1) * CHUNK] = turned

        @pl.when(chunk >= y_chunks)
        def _():
            rows = pl.ds(pl.multiple_of(start - y_count, CHUNK), CHUNK)
            value_high, value_low = split(value)
            z_first[rows, 0:wide] = value_high
            z_first[rows, wide:] = jnp.where(low, value_low.astype(F32), 0.0).astype(BF16)
            both_high, both_low = split(both)
            z_lap[rows, 0:wide] = both_high
            z_lap[rows, wide : 2 * wide] = both_high
            z_lap[rows, 2 * wide :] = both_low
            z_high[rows, 0:wide] = both_high
            z_high[rows, wide:] = both_low
            z_low[rows] = both_high

        return carry

    lax.fori_loop(0, y_chunks + z_chunks, forward_chunk, 0)

    diffusivity = jnp.exp(jnp.full((8, CHUNK), physics[0], F32))
    d_row = diffusivity[0:1]
    peak_speed = physics[1]
    bend_rate = physics[2]
    z_at = offsets[2] + lax.broadcasted_iota(jnp.int32, (1, z_count), 1)
    z_line = (2 * z_at + 1).astype(F32) * (1.0 / z_whole) - 1.0
    z_square = z_line * z_line
    tile = 16
    d_field = jnp.broadcast_to(d_row[:, 0:1], (tile, z_count))

    def plane_rows(step, carry):
        start = pl.multiple_of(step * tile, tile)
        y_at = offsets[1] + start + lax.broadcasted_iota(jnp.int32, (tile, z_count), 0)
        y_line = (2 * y_at + 1).astype(F32) * (1.0 / y_whole) - 1.0
        y_square = y_line * y_line
        base = (1.0 - y_square) * (1.0 - z_square)
        spread = y_square + z_square
        profile = base * (1.0 + bend_rate * spread)
        rows = pl.ds(start, tile)
        profile_ref[rows] = profile
        speed_ref[rows] = peak_speed * profile
        shape_ref[rows] = base * spread
        return carry

    lax.fori_loop(0, y_count // tile, plane_rows, 0)
    sums[...] = jnp.zeros_like(sums)
    y_cot[...] = jnp.zeros_like(y_cot)
    z_turn[...] = jnp.zeros_like(z_turn)
    ylow = lax.broadcasted_iota(jnp.int32, (y_count, wide), 1) < rank

    def plane(index, carry):
        value_row = x_rows[index, :, 0:wide]
        slope_row = x_rows[index, :, wide : 2 * wide]
        curve_row = x_rows[index, :, 2 * wide :]
        for scale_row, target in ((value_row, u_ref), (slope_row, s_ref)):
            high, low_part = split(y_value[...] * scale_row)
            mixed = jnp.where(ylow, high.astype(F32), low_part.astype(F32)).astype(BF16)
            target[...] = product(jnp.concatenate([mixed, high], 1), z_first[...], LAST)
        pair_lap = jnp.where(ylow, y_swap[...] * value_row + y_value[...] * curve_row, y_value[...] * value_row)
        high, low_part = split(pair_lap)
        l_ref[...] = product(jnp.concatenate([high, low_part, high], 1), z_lap[...], LAST)

        def cells(step, inner):
            start = pl.multiple_of(step * tile, tile)
            rows = pl.ds(start, tile)
            along_x = s_ref[rows]
            laplace = l_ref[rows]
            speed = speed_ref[rows]
            residual = speed * along_x - d_field * laplace - source[index, rows].astype(F32)
            misfit = u_ref[rows] - observed[index, rows].astype(F32)
            drive = residual * along_x
            sums[0] += residual * residual + misfit * misfit
            sums[1] += residual * laplace
            sums[2] += drive * profile_ref[rows]
            sums[3] += drive * shape_ref[rows]
            for slot, field in enumerate((misfit, residual * speed, residual)):
                at = pl.ds(pl.multiple_of(slot * y_count + start, tile), tile)
                f_high[at], f_low[at] = split(field)
            return inner

        lax.fori_loop(0, y_count // tile, cells, 0, unroll=2)
        over_z = product(f_high[...], z_high[...], PLAIN)
        over_z = over_z[:, :wide] + over_z[:, wide:] + product(f_low[...], z_low[...], PLAIN)
        t_m = over_z[:y_count]
        t_w = over_z[y_count : 2 * y_count]
        t_r = over_z[2 * y_count :] * (-d_row)
        t_s = jnp.concatenate([t_r[:, rank:], t_r[:, :rank]], 1)
        y_cot[0:y_count] += (
            jnp.where(ylow, value_row * t_m + slope_row * t_w + curve_row * t_r, 0.0) + value_row * t_s
        )
        y_low = y_both[...]
        x_cot[index, :, 0:wide] = row_sum(t_m * y_low)
        x_cot[index, :, wide : 2 * wide] = row_sum(t_w * y_low)
        x_cot[index, :, 2 * wide : 3 * wide] = row_sum(t_r * y_low)
        x_cot[index, :, 3 * wide :] = row_sum(t_r * y_swap[...])
        value_turn = y_turn[:rank]
        curve_turn = y_turn[rank:]
        columns = [
            jnp.concatenate([x_cols[index, slot * rank : (slot + 1) * rank]] * y_chunks, 1) for slot in range(3)
        ]
        scale = jnp.concatenate([jnp.broadcast_to(d_row, (rank, CHUNK))] * y_chunks, 1)
        pair_value = columns[0] * value_turn
        pair_curve = -scale * (columns[2] * value_turn + columns[0] * curve_turn)
        nothing = jnp.zeros((rank, y_count), F32)
        pairs = jnp.concatenate(
            [
                jnp.concatenate([pair_value, columns[1] * value_turn, pair_curve], 1),
                jnp.concatenate([nothing, nothing, -scale * pair_value], 1),
            ],
            0,
        )
        pair_high, pair_low = split(pairs)
        over_y = product(jnp.concatenate([pair_high, pair_low], 0), f_high[...], PLAIN)
        z_turn[...] += over_y[:wide] + over_y[wide:] + product(pair_high, f_low[...], PLAIN)
        return carry

    lax.fori_loop(0, x_count, plane, 0)

    factor = 2.0 / ncells
    depth = hidden_weight.shape[1]
    totals_row = 3 * depth * LANES + 3 * rank + 9 + 3 * depth
    spots = lax.broadcasted_iota(jnp.int32, (1, CHUNK), 1)
    totals = [jnp.sum(row_sum(sums[slot]), 1, keepdims=True) for slot in range(4)]
    out_ref[pl.ds(totals_row, 1), pl.ds(0, CHUNK)] = (
        jnp.where(spots == 0, totals[0] / ncells, 0.0)
        + jnp.where(spots == 1, -factor * d_row * totals[1], 0.0)
        + jnp.where(spots == 2, factor * totals[2], 0.0)
        + jnp.where(spots == 3, factor * peak_speed * totals[3], 0.0)
    )

    x_low = lax.broadcasted_iota(jnp.int32, (x_count, wide), 1) < rank
    x_cot_all = jnp.concatenate([x_cot[row] for row in range(x_count)], 0)
    mixed = x_cot_all[:, 3 * wide :]
    mixed = mixed + jnp.concatenate([mixed[:, rank:], mixed[:, :rank]], 1)
    x_cots = [
        jnp.where(x_low, factor * part, 0.0)
        for part in (x_cot_all[:, 0:wide] + mixed, x_cot_all[:, wide : 2 * wide], x_cot_all[:, 2 * wide : 3 * wide])
    ]
    net_backward(0, x_points, x_base, x_count, refs, out_ref, small, x_cots, False, rank)

    def spread_z(chunk):
        return jnp.transpose(z_turn[:, chunk * CHUNK : (chunk + 1) * CHUNK])

    for chunk in range(z_chunks):
        y_cot[y_count + chunk * CHUNK : y_count + (chunk + 1) * CHUNK] = spread_z(chunk)

    def backward_chunk(chunk, carry):
        which = jnp.where(chunk >= y_chunks, 2, 1)
        start = pl.multiple_of(chunk * CHUNK, CHUNK)
        both = factor * y_cot[pl.ds(start, CHUNK)]
        net_backward(which, line_points(chunk), start, CHUNK, refs, out_ref, small, (both, None, both), True, rank)
        return carry

    lax.fori_loop(0, y_chunks + z_chunks, backward_chunk, 0)
    at_first = 3 * depth * LANES + 3 * rank
    for slot in range(9 + 3 * depth):
        out_ref[at_first + slot : at_first + slot + 1] = small[slot]


def step_terms(offsets, wholes, padded, source, observed, physics, first_weight, first_bias, hidden_weight, hidden_bias, final_weight, final_bias):
    x_count, y_count, z_count = source.shape
    rank = final_weight.shape[2]
    depth = hidden_weight.shape[1]
    wide = 2 * rank
    lines = y_count + z_count
    vmem = pl.BlockSpec(memory_space=pltpu.VMEM)
    smem = pl.BlockSpec(memory_space=pltpu.SMEM)
    plane = pltpu.VMEM((y_count, z_count), F32)
    return pl.pallas_call(
        functools.partial(step_kernel, wholes, rank),
        out_shape=jax.ShapeDtypeStruct((padded, LANES), F32),
        in_specs=[smem, smem] + [vmem] * 8,
        out_specs=vmem,
        scratch_shapes=[
            pltpu.VMEM((depth + 1, lines + x_count, LANES), F32),
            pltpu.VMEM((depth, lines + x_count, LANES), F32),
            pltpu.VMEM((depth, lines + x_count, LANES), F32),
            pltpu.VMEM((x_count, 1, 3 * wide), F32),
            pltpu.VMEM((x_count, 3 * rank, CHUNK), F32),
            pltpu.VMEM((y_count, wide), F32),
            pltpu.VMEM((y_count, wide), F32),
            pltpu.VMEM((y_count, wide), F32),
            pltpu.VMEM((wide, y_count), F32),
            pltpu.VMEM((z_count, 2 * wide), BF16),
            pltpu.VMEM((z_count, 3 * wide), BF16),
            pltpu.VMEM((z_count, 2 * wide), BF16),
            pltpu.VMEM((z_count, wide), BF16),
            plane,
            plane,
            plane,
            plane,
            plane,
            plane,
            pltpu.VMEM((3 * y_count, z_count), BF16),
            pltpu.VMEM((3 * y_count, z_count), BF16),
            pltpu.VMEM((x_count, 1, 4 * wide), F32),
            pltpu.VMEM((lines, wide), F32),
            pltpu.VMEM((wide, z_count), F32),
            pltpu.VMEM((4, 16, z_count), F32),
            pltpu.VMEM((9 + 3 * depth, 1, LANES), F32),
        ],
        compiler_params=pltpu.CompilerParams(vmem_limit_bytes=52 << 20),
    )(
        offsets,
        physics,
        source,
        observed,
        first_weight.reshape(3, 1, LANES),
        first_bias.reshape(3, 1, LANES),
        hidden_weight,
        hidden_bias.reshape(3 * depth, 1, LANES),
        jnp.concatenate([final_weight, final_weight], 2),
        jnp.concatenate([final_bias, final_bias], 1).reshape(3, 1, wide),
    )


def local(source, observed, physics, first_weight, first_bias, hidden_weight, hidden_bias, final_weight, final_bias):
    sizes = {name: lax.axis_size(name) for name in ("gx", "gy", "gz")}
    wholes = tuple(count * size for count, size in zip(source.shape, sizes.values()))
    offsets = jnp.stack([lax.axis_index(name) * count for name, count in zip(sizes, source.shape)]).astype(jnp.int32)
    rank = final_weight.shape[2]
    depth = hidden_weight.shape[1]
    at_final = 3 * depth * LANES
    at_first = at_final + 3 * rank
    rows = at_first + 10 + 3 * depth
    padded, channels = reduce_plan(rows, sizes)
    packed = step_terms(
        offsets, wholes, padded, source, observed, physics, first_weight, first_bias,
        hidden_weight, hidden_bias, final_weight, final_bias,
    )
    summed = all_reduce(packed, channels, sizes)
    at_bias = at_first + 6 + 3 * depth
    return (
        summed[rows - 1, 0],
        summed[rows - 1, 1:4],
        summed[at_first : at_first + 3],
        summed[at_first + 3 : at_first + 6],
        summed[:at_final].reshape(hidden_weight.shape),
        summed[at_first + 6 : at_bias].reshape(hidden_bias.shape),
        jnp.swapaxes(summed[at_final:at_first].reshape(3, rank, LANES), 1, 2),
        summed[at_bias : at_bias + 3, :rank],
    )


def solution(mesh):
    in_specs = (P("gx", "gy", "gz"), P("gx", "gy", "gz"), P(), P(), P(), P(), P(), P(), P())
    out_specs = (P(), P(), P(), P(), P(), P(), P(), P())
    return jax.shard_map(local, mesh=mesh, in_specs=in_specs, out_specs=out_specs, check_vma=False)
```

```python
import functools
import jax
import jax.numpy as jnp
from jax import lax
from jax.experimental import pallas as pl
from jax.experimental.pallas import tpu as pltpu
from jax.sharding import PartitionSpec as P

HIGHEST = lax.Precision.HIGHEST
CHUNK = 128

LANES = 256
MESH_ID = pl.DeviceIdType.MESH


def reduce_plan(total_rows, sizes):
    devices = 1
    for size in sizes.values():
        devices *= size
    unit = 8 * devices
    units = -(-total_rows // unit)
    lead = max(1, (units * 7 + 5) // 10)
    if lead == units and units > 1:
        lead -= 1
    front = (lead + 1) // 2
    channels = [(0, front * unit, ("gz", "gy", "gx"))]
    if units > lead:
        channels.append((lead * unit, (units - lead) * unit, ("gz", "gx", "gy")))
    if lead > front:
        channels.append((front * unit, (lead - front) * unit, ("gz", "gy", "gx")))
    return units * unit, channels


def all_reduce_body(channels, sizes, in_ref, out_ref, recv_refs, work_refs, sems):
    places = {name: lax.axis_index(name) for name in sizes}

    def partner(name, step):
        return {name: lax.rem(places[name] + step, sizes[name])}

    phases = len(sizes)
    sources = [in_ref] * len(channels)
    starts = [first for first, _, _ in channels]
    lengths = [rows for _, rows, _ in channels]
    bases = [first for first, _, _ in channels]
    history = [[] for _ in channels]
    flights = [[] for _ in channels]

    def scatter(slot, phase):
        name = channels[slot][2][phase]
        part = lengths[slot] // sizes[name]
        for step in range(1, sizes[name]):
            peer = lax.rem(places[name] + step, sizes[name])
            copy = pltpu.make_async_remote_copy(
                src_ref=sources[slot].at[pl.ds(pl.multiple_of(starts[slot] + peer * part, 8), part)],
                dst_ref=recv_refs[slot][phase].at[step - 1],
                send_sem=sems[slot][0].at[phase, step - 1],
                recv_sem=sems[slot][1].at[phase, step - 1],
                device_id=partner(name, step),
                device_id_type=MESH_ID,
            )
            copy.start()
            flights[slot].append(copy)

    def settle(slot):
        for copy in flights[slot]:
            copy.wait()
        flights[slot] = []

    def add_up(slot, phase):
        name = channels[slot][2][phase]
        part = lengths[slot] // sizes[name]
        value = sources[slot][pl.ds(pl.multiple_of(starts[slot] + places[name] * part, 8), part)]
        for step in range(1, sizes[name]):
            value = value + recv_refs[slot][phase][step - 1]
        history[slot].append((name, bases[slot], part))
        bases[slot] = pl.multiple_of(bases[slot] + places[name] * part, 8)
        if phase == phases - 1:
            out_ref[pl.ds(bases[slot], part)] = value
        else:
            work_refs[slot][phase][...] = value
            sources[slot] = work_refs[slot][phase]
            starts[slot] = 0
        lengths[slot] = part

    def gather(slot, phase):
        name, base, part = history[slot][phase]
        mine = out_ref.at[pl.ds(pl.multiple_of(base + places[name] * part, 8), part)]
        for step in range(1, sizes[name]):
            copy = pltpu.make_async_remote_copy(
                src_ref=mine,
                dst_ref=mine,
                send_sem=sems[slot][2].at[phase, step - 1],
                recv_sem=sems[slot][3].at[phase, step - 1],
                device_id=partner(name, step),
                device_id_type=MESH_ID,
            )
            copy.start()
            flights[slot].append(copy)

    for turn in range(2 * phases + 1):
        for slot in range(len(channels)):
            settle(slot)
            if 0 < turn <= phases:
                add_up(slot, turn - 1)
            if turn < phases:
                scatter(slot, turn)
            elif turn < 2 * phases:
                gather(slot, 2 * phases - 1 - turn)


def entry_barrier(sizes):
    barrier = pltpu.get_barrier_semaphore()
    count = 0
    for name, size in sizes.items():
        for step in range(1, size):
            peer = lax.rem(lax.axis_index(name) + step, size)
            pl.semaphore_signal(barrier, inc=1, device_id={name: peer}, device_id_type=MESH_ID)
            count += 1
    pl.semaphore_wait(barrier, count)


def reduce_scratch(channels, sizes):
    scratch = []
    widest = max(sizes.values())
    for _, rows, order in channels:
        for name in order:
            rows //= sizes[name]
            scratch.append(pltpu.VMEM((sizes[name] - 1, rows, LANES), jnp.float32))
            scratch.append(pltpu.VMEM((rows, LANES), jnp.float32))
        for _ in range(4):
            scratch.append(pltpu.SemaphoreType.DMA((len(sizes), widest - 1)))
    return scratch


def split_scratch(channels, sizes, refs):
    phases = len(sizes)
    each = 2 * phases + 4
    recv_refs, work_refs, sems = [], [], []
    for slot in range(len(channels)):
        group = refs[slot * each : (slot + 1) * each]
        recv_refs.append(group[0 : 2 * phases : 2])
        work_refs.append(group[1 : 2 * phases : 2])
        sems.append(group[2 * phases :])
    return recv_refs, work_refs, sems


def reduce_kernel(channels, sizes, in_ref, out_ref, *scratch):
    entry_barrier(sizes)
    all_reduce_body(channels, sizes, in_ref, out_ref, *split_scratch(channels, sizes, scratch))


def all_reduce(packed, channels, sizes):
    return pl.pallas_call(
        functools.partial(reduce_kernel, channels, sizes),
        out_shape=jax.ShapeDtypeStruct(packed.shape, jnp.float32),
        in_specs=[pl.BlockSpec(memory_space=pltpu.VMEM)],
        out_specs=pl.BlockSpec(memory_space=pltpu.VMEM),
        scratch_shapes=reduce_scratch(channels, sizes),
        compiler_params=pltpu.CompilerParams(collective_id=0, has_side_effects=True, vmem_limit_bytes=24 << 20),
    )(packed)


F32 = jnp.float32
BF16 = jnp.bfloat16


def split(value):
    high = value.astype(BF16)
    return high, (value - high.astype(F32)).astype(BF16)


def product(left, right, dims):
    return lax.dot_general(left, right, (dims, ((), ())), preferred_element_type=F32)


def three_pass(left, right, dims):
    left_high, left_low = left
    right_high, right_low = right
    return (
        product(left_high, right_high, dims)
        + product(left_low, right_high, dims)
        + product(left_high, right_low, dims)
    )


LAST = ((1,), (1,))
FIRST = ((0,), (0,))
PLAIN = ((1,), (0,))


def tanh_jet(hidden, pre_slope, pre_curve):
    damping = 1.0 - hidden * hidden
    slope = damping * pre_slope
    if pre_curve is None:
        return slope, -2.0 * hidden * damping * (pre_slope * pre_slope)
    return slope, damping * pre_curve - 2.0 * hidden * damping * pre_slope * pre_slope


def tanh_jet_back(hidden, pre_slope, pre_curve, d_value, d_slope, d_curve):
    damping = 1.0 - hidden * hidden
    square = pre_slope * pre_slope
    d_pre_curve = damping * d_curve
    d_pre_slope = -4.0 * hidden * pre_slope * d_pre_curve
    bend = -2.0 * hidden * square
    if pre_curve is not None:
        bend = bend + pre_curve
    d_damping = bend * d_curve
    if d_slope is not None:
        d_pre_slope = d_pre_slope + damping * d_slope
        d_damping = d_damping + pre_slope * d_slope
    d_pre = damping * (d_value - 2.0 * square * d_pre_curve - 2.0 * hidden * d_damping)
    return d_pre, d_pre_slope, d_pre_curve


def points_column(offset, count, whole):
    position = offset + lax.broadcasted_iota(jnp.int32, (count, LANES), 0)
    return (2 * position + 1).astype(F32) * (1.0 / whole) - 1.0


def net_forward(which, points, first_row, count, refs):
    first_weight, first_bias, hidden_weight, hidden_bias, twice, bias_twice, hid, slo, cur = refs
    rows = pl.ds(first_row, count)
    weight = first_weight[which]
    hidden = jnp.tanh(points * weight + first_bias[which])
    hid[0, rows] = hidden
    slope, curve = tanh_jet(hidden, weight, None)
    depth = hidden_weight.shape[1]
    for layer in range(depth):
        stacked = jnp.dot(
            jnp.concatenate([hidden, slope, curve], 0),
            hidden_weight[which, layer],
            precision=HIGHEST,
            preferred_element_type=F32,
        )
        pre_slope = stacked[count : 2 * count]
        pre_curve = stacked[2 * count :]
        hidden = jnp.tanh(stacked[:count] + hidden_bias[which * depth + layer])
        hid[layer + 1, rows] = hidden
        slo[layer, rows] = pre_slope
        cur[layer, rows] = pre_curve
        slope, curve = tanh_jet(hidden, pre_slope, pre_curve)
    stacked = jnp.dot(
        jnp.concatenate([hidden, slope, curve], 0), twice[which], precision=HIGHEST, preferred_element_type=F32
    )
    return (
        stacked[:count] + bias_twice[which],
        stacked[count : 2 * count],
        stacked[2 * count :],
    )


def row_sum(value):
    return jnp.sum(value, 0, keepdims=True)


def net_backward(which, points, first_row, count, refs, out_ref, small, cotangents, packed, rank):
    first_weight, first_bias, hidden_weight, hidden_bias, twice, bias_twice, hid, slo, cur = refs
    depth = hidden_weight.shape[1]
    width = LANES
    rows = pl.ds(first_row, count)
    at_final = 3 * depth * width
    lane = lax.broadcasted_iota(jnp.int32, (width, 2 * rank), 1)
    low_weight = split(jnp.where(lane < rank, twice[which], 0.0))
    high_weight = split(jnp.where(lane >= rank, twice[which], 0.0)) if packed else low_weight
    hidden = hid[depth, rows]
    pre_slope = slo[depth - 1, rows]
    pre_curve = cur[depth - 1, rows]
    slope, curve = tanh_jet(hidden, pre_slope, pre_curve)
    parts = [None if cot is None else split(cot) for cot in cotangents]
    grad = three_pass(parts[0], split(hidden), FIRST)[:rank]
    curve_grad = three_pass(parts[2], split(curve), FIRST)
    grad = grad + (curve_grad[rank:] if packed else curve_grad[:rank])
    d_value = three_pass(parts[0], low_weight, LAST)
    d_curve = three_pass(parts[2], high_weight, LAST)
    d_slope = None
    if parts[1] is not None:
        grad = grad + three_pass(parts[1], split(slope), FIRST)[:rank]
        d_slope = three_pass(parts[1], low_weight, LAST)
    out_ref[pl.ds(pl.multiple_of(at_final + which * rank, 8), rank)] += grad
    biases = row_sum(cotangents[0])
    small[6 + 3 * depth + which, :, 0 : 2 * rank] += biases
    for layer in reversed(range(depth)):
        steps = tanh_jet_back(hidden, pre_slope, pre_curve, d_value, d_slope, d_curve)
        small[6 + which * depth + layer] += row_sum(steps[0])
        hidden = hid[layer, rows]
        if layer:
            pre_slope = slo[layer - 1, rows]
            pre_curve = cur[layer - 1, rows]
        else:
            pre_slope = first_weight[which]
            pre_curve = None
        slope, curve = tanh_jet(hidden, pre_slope, pre_curve)
        deltas = split(jnp.concatenate(steps, 0))
        acts = split(jnp.concatenate([hidden, slope, curve], 0))
        out_ref[pl.ds(pl.multiple_of((which * depth + layer) * width, 8), width)] += three_pass(acts, deltas, FIRST)
        back = three_pass(deltas, split(hidden_weight[which, layer]), LAST)
        d_value, d_slope, d_curve = back[:count], back[count : 2 * count], back[2 * count :]
    steps = tanh_jet_back(hidden, pre_slope, None, d_value, d_slope, d_curve)
    small[which] += row_sum(points * steps[0] + steps[1])
    small[3 + which] += row_sum(steps[0])


def step_kernel(
    wholes,
    rank,
    offsets,
    physics,
    source_any,
    observed_any,
    first_weight_in_any,
    first_bias_in_any,
    hidden_weight_any,
    hidden_bias_in_any,
    final_weight_any,
    final_bias_any,
    out_ref,
    hid,
    slo,
    cur,
    x_rows,
    x_cols,
    y_value,
    y_both,
    y_swap,
    y_turn,
    z_first,
    z_lap,
    z_high,
    z_low,
    speed_ref,
    profile_ref,
    shape_ref,
    u_ref,
    s_ref,
    l_ref,
    f_high,
    f_low,
    x_cot,
    y_cot,
    z_turn,
    sums,
    small,
    first_weight,
    first_bias,
    hidden_bias,
    twice,
    bias_twice,
    source,
    observed,
    first_weight_in,
    first_bias_in,
    hidden_weight,
    hidden_bias_in,
    final_weight,
    final_bias,
    arrived,
):
    fetches = [
        pltpu.make_async_copy(here, there, arrived.at[slot])
        for slot, (here, there) in enumerate(
            [
                (first_weight_in_any, first_weight_in),
                (first_bias_in_any, first_bias_in),
                (hidden_weight_any, hidden_weight),
                (hidden_bias_in_any, hidden_bias_in),
                (final_weight_any, final_weight),
                (final_bias_any, final_bias),
                (source_any, source),
                (observed_any, observed),
            ]
        )
    ]
    for fetch in fetches:
        fetch.start()
    out_ref[...] = jnp.zeros_like(out_ref)
    small[...] = jnp.zeros_like(small)
    for fetch in fetches[:6]:
        fetch.wait()
    refs = (first_weight, first_bias, hidden_weight, hidden_bias, twice, bias_twice, hid, slo, cur)
    for net in range(3):
        first_weight[net] = first_weight_in[net : net + 1]
        first_bias[net] = first_bias_in[net : net + 1]
        for layer in range(hidden_weight.shape[1]):
            hidden_bias[net * hidden_weight.shape[1] + layer] = hidden_bias_in[net, layer : layer + 1]
        twice[net] = jnp.transpose(jnp.concatenate([final_weight[net], final_weight[net]], 0))
        bias_twice[net] = jnp.concatenate([final_bias[net : net + 1], final_bias[net : net + 1]], 1)
    x_count, y_count, z_count = source.shape
    x_whole, y_whole, z_whole = wholes
    ncells = float(x_whole * y_whole * z_whole)
    wide = 2 * rank
    y_chunks = y_count // CHUNK
    z_chunks = z_count // CHUNK
    x_base = y_count + z_count
    lane = lax.broadcasted_iota(jnp.int32, (CHUNK, wide), 1)
    low = lane < rank

    def line_points(chunk):
        on_z = chunk >= y_chunks
        first = jnp.where(on_z, offsets[2] + (chunk - y_chunks) * CHUNK, offsets[1] + chunk * CHUNK)
        scale = jnp.where(on_z, F32(1.0 / z_whole), F32(1.0 / y_whole))
        position = first + lax.broadcasted_iota(jnp.int32, (CHUNK, LANES), 0)
        return (2 * position + 1).astype(F32) * scale - 1.0

    x_points = points_column(offsets[0], x_count, x_whole)
    x_jets = net_forward(0, x_points, x_base, x_count, refs)
    for slot in range(3):
        for row in range(x_count):
            x_rows[row, :, slot * wide : (slot + 1) * wide] = x_jets[slot][row : row + 1]
    for slot in range(3):
        turned = jnp.transpose(
            jnp.concatenate([x_jets[slot], jnp.zeros((CHUNK - x_count, wide), F32)], 0)
        )
        for row in range(x_count):
            x_cols[row, slot * rank : (slot + 1) * rank] = jnp.broadcast_to(
                turned[:rank, row : row + 1], (rank, CHUNK)
            )

    def forward_chunk(chunk, carry):
        which = jnp.where(chunk >= y_chunks, 2, 1)
        start = pl.multiple_of(chunk * CHUNK, CHUNK)
        value, _, curve = net_forward(which, line_points(chunk), start, CHUNK, refs)
        both = jnp.where(low, value, curve)

        @pl.when(chunk < y_chunks)
        def _():
            rows = pl.ds(start, CHUNK)
            y_value[rows] = value
            y_both[rows] = both
            y_swap[rows] = jnp.where(low, curve, value)
            turned = jnp.transpose(both)
            for half in range(y_chunks):
                @pl.when(chunk == half)
                def _():
                    y_turn[:, half * CHUNK : (half + 1) * CHUNK] = turned

        @pl.when(chunk >= y_chunks)
        def _():
            rows = pl.ds(pl.multiple_of(start - y_count, CHUNK), CHUNK)
            value_high, value_low = split(value)
            z_first[rows, 0:wide] = value_high
            z_first[rows, wide:] = jnp.where(low, value_low.astype(F32), 0.0).astype(BF16)
            both_high, both_low = split(both)
            z_lap[rows, 0:wide] = both_high
            z_lap[rows, wide : 2 * wide] = both_high
            z_lap[rows, 2 * wide :] = both_low
            z_high[rows, 0:wide] = both_high
            z_high[rows, wide:] = both_low
            z_low[rows] = both_high

        return carry

    lax.fori_loop(0, y_chunks + z_chunks, forward_chunk, 0)

    diffusivity = jnp.exp(jnp.full((8, CHUNK), physics[0], F32))
    d_row = diffusivity[0:1]
    peak_speed = physics[1]
    bend_rate = physics[2]
    z_at = offsets[2] + lax.broadcasted_iota(jnp.int32, (1, z_count), 1)
    z_line = (2 * z_at + 1).astype(F32) * (1.0 / z_whole) - 1.0
    z_square = z_line * z_line
    tile = 16
    d_field = jnp.broadcast_to(d_row[:, 0:1], (tile, z_count))

    def plane_rows(step, carry):
        start = pl.multiple_of(step * tile, tile)
        y_at = offsets[1] + start + lax.broadcasted_iota(jnp.int32, (tile, z_count), 0)
        y_line = (2 * y_at + 1).astype(F32) * (1.0 / y_whole) - 1.0
        y_square = y_line * y_line
        base = (1.0 - y_square) * (1.0 - z_square)
        spread = y_square + z_square
        profile = base * (1.0 + bend_rate * spread)
        rows = pl.ds(start, tile)
        profile_ref[rows] = profile
        speed_ref[rows] = peak_speed * profile
        shape_ref[rows] = base * spread
        return carry

    lax.fori_loop(0, y_count // tile, plane_rows, 0)
    sums[...] = jnp.zeros_like(sums)
    y_cot[...] = jnp.zeros_like(y_cot)
    z_turn[...] = jnp.zeros_like(z_turn)
    ylow = lax.broadcasted_iota(jnp.int32, (y_count, wide), 1) < rank

    def plane(index, carry):
        value_row = x_rows[index, :, 0:wide]
        slope_row = x_rows[index, :, wide : 2 * wide]
        curve_row = x_rows[index, :, 2 * wide :]
        for scale_row, target in ((value_row, u_ref), (slope_row, s_ref)):
            high, low_part = split(y_value[...] * scale_row)
            mixed = jnp.where(ylow, high.astype(F32), low_part.astype(F32)).astype(BF16)
            target[...] = product(jnp.concatenate([mixed, high], 1), z_first[...], LAST)
        pair_lap = jnp.where(ylow, y_swap[...] * value_row + y_value[...] * curve_row, y_value[...] * value_row)
        high, low_part = split(pair_lap)
        l_ref[...] = product(jnp.concatenate([high, low_part, high], 1), z_lap[...], LAST)

        def cells(step, inner):
            start = pl.multiple_of(step * tile, tile)
            rows = pl.ds(start, tile)
            along_x = s_ref[rows]
            laplace = l_ref[rows]
            speed = speed_ref[rows]
            residual = speed * along_x - d_field * laplace - source[index, rows].astype(F32)
            misfit = u_ref[rows] - observed[index, rows].astype(F32)
            drive = residual * along_x
            sums[0] += residual * residual + misfit * misfit
            sums[1] += residual * laplace
            sums[2] += drive * profile_ref[rows]
            sums[3] += drive * shape_ref[rows]
            for slot, field in enumerate((misfit, residual * speed, residual)):
                at = pl.ds(pl.multiple_of(slot * y_count + start, tile), tile)
                f_high[at], f_low[at] = split(field)
            return inner

        lax.fori_loop(0, y_count // tile, cells, 0, unroll=2)
        over_z = product(f_high[...], z_high[...], PLAIN)
        over_z = over_z[:, :wide] + over_z[:, wide:] + product(f_low[...], z_low[...], PLAIN)
        t_m = over_z[:y_count]
        t_w = over_z[y_count : 2 * y_count]
        t_r = over_z[2 * y_count :] * (-d_row)
        t_s = jnp.concatenate([t_r[:, rank:], t_r[:, :rank]], 1)
        y_cot[0:y_count] += (
            jnp.where(ylow, value_row * t_m + slope_row * t_w + curve_row * t_r, 0.0) + value_row * t_s
        )
        y_low = y_both[...]
        x_cot[index, :, 0:wide] = row_sum(t_m * y_low)
        x_cot[index, :, wide : 2 * wide] = row_sum(t_w * y_low)
        x_cot[index, :, 2 * wide : 3 * wide] = row_sum(t_r * y_low)
        x_cot[index, :, 3 * wide :] = row_sum(t_r * y_swap[...])
        value_turn = y_turn[:rank]
        curve_turn = y_turn[rank:]
        columns = [
            jnp.concatenate([x_cols[index, slot * rank : (slot + 1) * rank]] * y_chunks, 1) for slot in range(3)
        ]
        scale = jnp.concatenate([jnp.broadcast_to(d_row, (rank, CHUNK))] * y_chunks, 1)
        pair_value = columns[0] * value_turn
        pair_curve = -scale * (columns[2] * value_turn + columns[0] * curve_turn)
        nothing = jnp.zeros((rank, y_count), F32)
        pairs = jnp.concatenate(
            [
                jnp.concatenate([pair_value, columns[1] * value_turn, pair_curve], 1),
                jnp.concatenate([nothing, nothing, -scale * pair_value], 1),
            ],
            0,
        )
        pair_high, pair_low = split(pairs)
        over_y = product(jnp.concatenate([pair_high, pair_low], 0), f_high[...], PLAIN)
        z_turn[...] += over_y[:wide] + over_y[wide:] + product(pair_high, f_low[...], PLAIN)
        return carry

    for fetch in fetches[6:]:
        fetch.wait()
    lax.fori_loop(0, x_count, plane, 0)

    factor = 2.0 / ncells
    depth = hidden_weight.shape[1]
    totals_row = 3 * depth * LANES + 3 * rank + 9 + 3 * depth
    spots = lax.broadcasted_iota(jnp.int32, (1, CHUNK), 1)
    totals = [jnp.sum(row_sum(sums[slot]), 1, keepdims=True) for slot in range(4)]
    out_ref[pl.ds(totals_row, 1), pl.ds(0, CHUNK)] = (
        jnp.where(spots == 0, totals[0] / ncells, 0.0)
        + jnp.where(spots == 1, -factor * d_row * totals[1], 0.0)
        + jnp.where(spots == 2, factor * totals[2], 0.0)
        + jnp.where(spots == 3, factor * peak_speed * totals[3], 0.0)
    )

    x_low = lax.broadcasted_iota(jnp.int32, (x_count, wide), 1) < rank
    x_cot_all = jnp.concatenate([x_cot[row] for row in range(x_count)], 0)
    mixed = x_cot_all[:, 3 * wide :]
    mixed = mixed + jnp.concatenate([mixed[:, rank:], mixed[:, :rank]], 1)
    x_cots = [
        jnp.where(x_low, factor * part, 0.0)
        for part in (x_cot_all[:, 0:wide] + mixed, x_cot_all[:, wide : 2 * wide], x_cot_all[:, 2 * wide : 3 * wide])
    ]
    net_backward(0, x_points, x_base, x_count, refs, out_ref, small, x_cots, False, rank)

    def spread_z(chunk):
        return jnp.transpose(z_turn[:, chunk * CHUNK : (chunk + 1) * CHUNK])

    for chunk in range(z_chunks):
        y_cot[y_count + chunk * CHUNK : y_count + (chunk + 1) * CHUNK] = spread_z(chunk)

    def backward_chunk(chunk, carry):
        which = jnp.where(chunk >= y_chunks, 2, 1)
        start = pl.multiple_of(chunk * CHUNK, CHUNK)
        both = factor * y_cot[pl.ds(start, CHUNK)]
        net_backward(which, line_points(chunk), start, CHUNK, refs, out_ref, small, (both, None, both), True, rank)
        return carry

    lax.fori_loop(0, y_chunks + z_chunks, backward_chunk, 0)
    at_first = 3 * depth * LANES + 3 * rank
    for slot in range(9 + 3 * depth):
        out_ref[at_first + slot : at_first + slot + 1] = small[slot]


def step_terms(offsets, wholes, padded, source, observed, physics, first_weight, first_bias, hidden_weight, hidden_bias, final_weight, final_bias):
    x_count, y_count, z_count = source.shape
    rank = final_weight.shape[2]
    depth = hidden_weight.shape[1]
    wide = 2 * rank
    lines = y_count + z_count
    vmem = pl.BlockSpec(memory_space=pltpu.VMEM)
    smem = pl.BlockSpec(memory_space=pltpu.SMEM)
    plane = pltpu.VMEM((y_count, z_count), F32)
    return pl.pallas_call(
        functools.partial(step_kernel, wholes, rank),
        out_shape=jax.ShapeDtypeStruct((padded, LANES), F32),
        in_specs=[smem, smem] + [pl.BlockSpec(memory_space=pl.ANY)] * 8,
        out_specs=vmem,
        scratch_shapes=[
            pltpu.VMEM((depth + 1, lines + x_count, LANES), F32),
            pltpu.VMEM((depth, lines + x_count, LANES), F32),
            pltpu.VMEM((depth, lines + x_count, LANES), F32),
            pltpu.VMEM((x_count, 1, 3 * wide), F32),
            pltpu.VMEM((x_count, 3 * rank, CHUNK), F32),
            pltpu.VMEM((y_count, wide), F32),
            pltpu.VMEM((y_count, wide), F32),
            pltpu.VMEM((y_count, wide), F32),
            pltpu.VMEM((wide, y_count), F32),
            pltpu.VMEM((z_count, 2 * wide), BF16),
            pltpu.VMEM((z_count, 3 * wide), BF16),
            pltpu.VMEM((z_count, 2 * wide), BF16),
            pltpu.VMEM((z_count, wide), BF16),
            plane,
            plane,
            plane,
            plane,
            plane,
            plane,
            pltpu.VMEM((3 * y_count, z_count), BF16),
            pltpu.VMEM((3 * y_count, z_count), BF16),
            pltpu.VMEM((x_count, 1, 4 * wide), F32),
            pltpu.VMEM((lines, wide), F32),
            pltpu.VMEM((wide, z_count), F32),
            pltpu.VMEM((4, 16, z_count), F32),
            pltpu.VMEM((9 + 3 * depth, 1, LANES), F32),
            pltpu.VMEM((3, 1, LANES), F32),
            pltpu.VMEM((3, 1, LANES), F32),
            pltpu.VMEM((3 * depth, 1, LANES), F32),
            pltpu.VMEM((3, LANES, wide), F32),
            pltpu.VMEM((3, 1, wide), F32),
            pltpu.VMEM(source.shape, BF16),
            pltpu.VMEM(observed.shape, BF16),
            pltpu.VMEM(first_weight.shape, F32),
            pltpu.VMEM(first_bias.shape, F32),
            pltpu.VMEM(hidden_weight.shape, F32),
            pltpu.VMEM(hidden_bias.shape, F32),
            pltpu.VMEM((3, rank, LANES), F32),
            pltpu.VMEM(final_bias.shape, F32),
            pltpu.SemaphoreType.DMA((8,)),
        ],
        compiler_params=pltpu.CompilerParams(vmem_limit_bytes=56 << 20),
    )(
        offsets,
        physics,
        source,
        observed,
        first_weight,
        first_bias,
        hidden_weight,
        hidden_bias,
        jnp.swapaxes(final_weight, 1, 2),
        final_bias,
    )


def local(source, observed, physics, first_weight, first_bias, hidden_weight, hidden_bias, final_weight, final_bias):
    sizes = {name: lax.axis_size(name) for name in ("gx", "gy", "gz")}
    wholes = tuple(count * size for count, size in zip(source.shape, sizes.values()))
    offsets = jnp.stack([lax.axis_index(name) * count for name, count in zip(sizes, source.shape)]).astype(jnp.int32)
    rank = final_weight.shape[2]
    depth = hidden_weight.shape[1]
    at_final = 3 * depth * LANES
    at_first = at_final + 3 * rank
    rows = at_first + 10 + 3 * depth
    padded, channels = reduce_plan(rows, sizes)
    packed = step_terms(
        offsets, wholes, padded, source, observed, physics, first_weight, first_bias,
        hidden_weight, hidden_bias, final_weight, final_bias,
    )
    summed = all_reduce(packed, channels, sizes)
    at_bias = at_first + 6 + 3 * depth
    return (
        summed[rows - 1, 0],
        summed[rows - 1, 1:4],
        summed[at_first : at_first + 3],
        summed[at_first + 3 : at_first + 6],
        summed[:at_final].reshape(hidden_weight.shape),
        summed[at_first + 6 : at_bias].reshape(hidden_bias.shape),
        jnp.swapaxes(summed[at_final:at_first].reshape(3, rank, LANES), 1, 2),
        summed[at_bias : at_bias + 3, :rank],
    )


def solution(mesh):
    in_specs = (P("gx", "gy", "gz"), P("gx", "gy", "gz"), P(), P(), P(), P(), P(), P(), P())
    out_specs = (P(), P(), P(), P(), P(), P(), P(), P())
    return jax.shard_map(local, mesh=mesh, in_specs=in_specs, out_specs=out_specs, check_vma=False)
```
